128 devices in a mesh: rows: 16 (over y, x), cols: 8 (over z, core).
Axes of the slice: x: 4, y: 4, z: 4, core: 2. Of those that a mesh axis runs over, the one named last changes fastest.
Arguments:
- slab: bfloat16 [4096, 262144], P('rows', 'cols')
- sign_bits: int32 [262144], P('cols'), may hold values from 0 to 1
- sampled: int32 [512], replicated, may hold values from 0 to 262143
Outputs:
- projected: float32 [512, 262144], P('rows', 'cols')
The draws below stay inside these ranges and needn't reach their ends.
All inputs are finite; a program needn't handle non-finite values.
Results may differ from the reference program's by a relative error of at most 0.0029.
Values may be sent and summed in bfloat16 or wider, within the bound.
No kernel may reach another device: no remote copies, remote signals or barrier semaphores. Data moves between devices by JAX's collectives and lax.ppermute only.
A program may use at most 256 MiB of HBM per device.

```python
import math
import jax
import jax.numpy as jnp
from jax import lax

N = 262144
K = 512
ROWS = 4096


def draw_slab(key, part):
    key = jax.random.fold_in(key, 11)
    knoise, krow, kcol = jax.random.split(key, 3)
    noise = jax.random.normal(knoise, (ROWS, N), jnp.float32)
    position = jnp.arange(ROWS, dtype=jnp.float32)
    rising = jnp.exp(math.log(10.0) * (position[:, None] + 0.5) / ROWS) * jnp.exp(jax.random.uniform(krow, (ROWS, 1), jnp.float32, -0.3, 0.3))
    column_scale = jnp.exp(jax.random.uniform(kcol, (1, N), jnp.float32, math.log(0.3), math.log(3.0)))
    return (noise * rising * column_scale * 0.2).astype(jnp.bfloat16)


def with_ends(values, rng, least, high):
    longest = values.shape.index(max(values.shape))
    spots = []
    for shift in (0, 1):
        where = [jax.random.randint(jax.random.fold_in(rng, axis), (), 0, length) for axis, length in enumerate(values.shape)]
        where[longest] = (where[longest] + shift) % values.shape[longest]
        spots.append(tuple(where))
    return values.at[spots[0]].set(least).at[spots[1]].set(high)


def setup_inputs(seed: int = 0) -> dict:
    keys = jax.random.split(jax.random.key(seed), 4)
    slab = draw_slab(jax.random.fold_in(keys[3], 71), 0)
    sign_bits = with_ends(jax.random.randint(keys[1], (N,), 0, 2), jax.random.fold_in(keys[1], 1), 0, 1).astype(jnp.int32)
    sampled = with_ends(jax.random.randint(keys[2], (K,), 0, N), jax.random.fold_in(keys[2], 1), 0, N - 1).astype(jnp.int32)
    return dict(slab=slab, sign_bits=sign_bits, sampled=sampled)


def parity_of(values, width):
    result = jnp.zeros_like(values)
    for shift_by in range(width):
        result = jnp.bitwise_xor(result, jnp.bitwise_and(jnp.right_shift(values, shift_by), 1))
    return result

def reference(slab, sign_bits, sampled):
    facet = jnp.arange(N, dtype=jnp.int32)
    masked = jnp.bitwise_and(facet[:, None], sampled[None, :])
    parity = parity_of(masked, N.bit_length())
    signed = (1 - 2 * parity) * (1 - 2 * sign_bits)[:, None]
    mixing = (signed.astype(jnp.float32) * (1.0 / math.sqrt(N))).astype(jnp.bfloat16)
    sketch = jnp.dot(slab, mixing, preferred_element_type=jnp.float32)
    squares = lax.optimization_barrier(jnp.sum(sketch * sketch, axis=0))
    basis = (sketch * lax.rsqrt(squares / ROWS + 1e-06)).astype(jnp.bfloat16)
    product = lax.dot_general(basis, slab, (((0,), (0,)), ((), ())), preferred_element_type=jnp.float32)
    return product * (1.0 / math.sqrt(ROWS))
```

```python
import math

import jax
import jax.numpy as jnp
from jax import lax
from jax.experimental import pallas as pl
from jax.experimental.pallas import tpu as pltpu
from jax.sharding import PartitionSpec as P

N = 262144
EPSILON = 1e-06
SIDE = 4
LOW = 1024
SKETCH_BLOCK = 4096
TILE = 512
WAVES = 2
DISTANCES = (1, 3, 2)
VMEM = 48 * 1024 * 1024


def x_perm(move):
    return [(y * SIDE + x, y * SIDE + move(x)) for y in range(SIDE) for x in range(SIDE)]


def y_perm(move):
    return [(y * SIDE + x, move(y) * SIDE + x) for y in range(SIDE) for x in range(SIDE)]


def parity_sign(values):
    for shift_by in (16, 8, 4, 2, 1):
        values = jnp.bitwise_xor(values, jnp.right_shift(values, shift_by))
    return (1 - 2 * jnp.bitwise_and(values, 1)).astype(jnp.float32)


def sketch_kernel(first_ref, slab_ref, bits_ref, sampled_ref, out_ref, low_ref, acc_ref):
    step = pl.program_id(0)
    sampled = sampled_ref[...]

    @pl.when(step == 0)
    def _():
        acc_ref[...] = jnp.zeros_like(acc_ref)
        column = lax.broadcasted_iota(jnp.int32, (sampled.shape[0], 128), 1)
        base = parity_sign(jnp.bitwise_and(column, sampled)) * (1.0 / math.sqrt(N))
        for part in range(LOW // 128):
            sign = parity_sign(jnp.bitwise_and(sampled, part * 128))
            low_ref[:, part * 128 : (part + 1) * 128] = (base * sign).astype(jnp.bfloat16)

    total = acc_ref[...]
    for part in range(SKETCH_BLOCK // LOW):
        where = slice(part * LOW, (part + 1) * LOW)
        flip = (1 - 2 * bits_ref[:, where]).astype(jnp.bfloat16)
        signed = slab_ref[:, where] * flip
        term = lax.dot_general(
            low_ref[...], signed, (((1,), (1,)), ((), ())), preferred_element_type=jnp.float32
        )
        high = first_ref[0] + step * SKETCH_BLOCK + part * LOW
        total = total + term * parity_sign(jnp.bitwise_and(sampled, high))
    acc_ref[...] = total

    @pl.when(step == pl.num_programs(0) - 1)
    def _():
        out_ref[...] = acc_ref[...]


def local_sketch(slab, sign_bits, sampled):
    rows, cols = slab.shape
    count = sampled.shape[0]
    first = (lax.axis_index("cols") * cols).astype(jnp.int32).reshape(1)
    return pl.pallas_call(
        sketch_kernel,
        grid_spec=pltpu.PrefetchScalarGridSpec(
            num_scalar_prefetch=1,
            grid=(cols // SKETCH_BLOCK,),
            in_specs=[
                pl.BlockSpec((rows, SKETCH_BLOCK), lambda i, s: (0, i)),
                pl.BlockSpec((1, SKETCH_BLOCK), lambda i, s: (0, i)),
                pl.BlockSpec((count, 1), lambda i, s: (0, 0)),
            ],
            out_specs=pl.BlockSpec((count, rows), lambda i, s: (0, 0)),
            scratch_shapes=[
                pltpu.VMEM((count, LOW), jnp.bfloat16),
                pltpu.VMEM((count, rows), jnp.float32),
            ],
        ),
        out_shape=jax.ShapeDtypeStruct((count, rows), jnp.float32),
        compiler_params=pltpu.CompilerParams(vmem_limit_bytes=VMEM),
        cost_estimate=pl.CostEstimate(
            flops=2 * count * rows * cols, bytes_accessed=2 * rows * cols, transcendentals=0
        ),
        name="sketch",
    )(first, slab, sign_bits.reshape(1, cols), sampled.reshape(count, 1))


def four_term_dot(basis, pieces):
    depth = pieces[0].shape[0]
    total = None
    for k, piece in enumerate(pieces):
        term = jnp.dot(
            basis[:, k * depth : (k + 1) * depth], piece[...], preferred_element_type=jnp.float32
        )
        total = term if total is None else total + term
    return total


def first_kernel(where_ref, low_ref, high_ref, p0, p1, p2, p3, out_ref):
    chunk = low_ref.shape[0]
    basis = jnp.concatenate([low_ref[...], high_ref[...]], axis=0)
    out_ref[...] = four_term_dot(basis, (p0, p1, p2, p3)).astype(out_ref.dtype)


def second_kernel(where_ref, basis_ref, p0, p1, p2, p3, got_ref, out_ref):
    total = four_term_dot(basis_ref[...], (p0, p1, p2, p3))
    out_ref[...] = (total + got_ref[...].astype(jnp.float32)).astype(out_ref.dtype)


def third_kernel(where_ref, basis_ref, p0, p1, p2, p3, ga1, ga2, gb1, gb2, own, o1, o2, o3, total_ref):
    total = four_term_dot(basis_ref[...], (p0, p1, p2, p3))
    is_a = pl.program_id(0) < pl.num_programs(0) // 2

    @pl.when(is_a)
    def _():
        total_ref[...] = total + ga1[...].astype(jnp.float32) + ga2[...].astype(jnp.float32)

    @pl.when(jnp.logical_not(is_a))
    def _():
        total_ref[...] = total + gb1[...].astype(jnp.float32) + gb2[...].astype(jnp.float32)

    height = own.shape[0]
    place = where_ref[4]
    own[...] = total_ref[pl.ds(pl.multiple_of(place * height, height), height), :]
    for out, distance in zip((o1, o2, o3), DISTANCES):
        row = lax.rem(place + distance, SIDE) * height
        out[...] = total_ref[pl.ds(pl.multiple_of(row, height), height), :].astype(out.dtype)


def product_call(kernel, name, where, out_shapes, out_specs, basis_specs, pieces, extra, extra_specs, tiles, column, basis, scratch=()):
    slab, received = pieces
    rows = slab.shape[0]
    piece_specs = [pl.BlockSpec((rows, TILE), lambda t, s: (0, s[5] + column + t))] + [
        pl.BlockSpec((rows, TILE), lambda t, s: (0, column + t)) for _ in received
    ]
    height = sum(spec.block_shape[0] for spec in basis_specs)
    depth = basis.shape[1]
    return pl.pallas_call(
        kernel,
        grid_spec=pltpu.PrefetchScalarGridSpec(
            num_scalar_prefetch=1,
            grid=(tiles,),
            in_specs=[*basis_specs, *piece_specs, *extra_specs],
            out_specs=out_specs,
            scratch_shapes=list(scratch),
        ),
        out_shape=out_shapes,
        compiler_params=pltpu.CompilerParams(vmem_limit_bytes=VMEM),
        cost_estimate=pl.CostEstimate(
            flops=2 * height * depth * tiles * TILE,
            bytes_accessed=2 * depth * (height + tiles * TILE),
            transcendentals=0,
        ),
        name=name,
    )(where, *([basis] * len(basis_specs)), slab, *received, *extra)


def assemble_kernel(where_ref, *refs):
    *pieces, out_ref = refs
    width = pieces[0].shape[1]
    scale = 1.0 / math.sqrt(4096)
    for group in range(len(pieces) // SIDE):
        place = where_ref[group % 2]
        for k, distance in enumerate((0,) + DISTANCES):
            piece = pieces[group * SIDE + k]
            source = lax.rem(place + SIDE - distance, SIDE)
            column = pl.multiple_of((group * SIDE + source) * width, width)
            out_ref[:, pl.ds(column, width)] = piece[...].astype(jnp.float32) * scale


def per_device(slab, sign_bits, sampled):
    rows, cols = slab.shape
    count = sampled.shape[0]
    col_devices = lax.axis_size("cols")
    total_rows = rows * lax.axis_size("rows")
    row_index = lax.axis_index("rows")
    y, x = row_index // SIDE, row_index % SIDE
    places = (x, y)
    perms = (x_perm, y_perm)
    width = cols // (WAVES * 2 * SIDE)
    half = width // 2
    chunk = count // SIDE

    received = {}
    for wave in range(WAVES):
        for axis in range(2):
            base = (wave * 2 + axis) * SIDE * width
            for distance in DISTANCES[::-1]:
                start = base + (places[axis] + distance) % SIDE * width
                block = lax.dynamic_slice(slab, (0, start), (rows, width))
                received[wave, axis, distance] = lax.ppermute(
                    block, "rows", perms[axis](lambda q: (q + distance) % SIDE)
                )

    partial = local_sketch(slab, sign_bits, sampled)
    share = count // col_devices
    parts = lax.all_to_all(partial, "cols", 0, 0, tiled=True)
    sketch = jnp.sum(parts.reshape(col_devices, share, rows), axis=0)
    local_squares = jnp.sum(sketch * sketch, axis=1)
    row_devices = lax.axis_size("rows")
    squares = jnp.sum(
        lax.all_to_all(jnp.broadcast_to(local_squares[None], (row_devices, share)), "rows", 0, 0, tiled=True), axis=0
    )
    basis = (sketch * lax.rsqrt(squares / total_rows + EPSILON)[:, None]).astype(jnp.bfloat16)

    finals = []
    bases = []
    for axis in range(2):
        terms = [basis] + [
            lax.ppermute(basis, "rows", perms[axis](lambda q: (q + distance) % SIDE)) for distance in DISTANCES
        ]
        joined = jnp.concatenate(terms, axis=1)
        whole = lax.all_to_all(jnp.tile(joined, (col_devices, 1)), "cols", 0, 0, tiled=True)
        if axis == 1:
            whole = whole.reshape(SIDE, SIDE, count // SIDE**2, -1).swapaxes(0, 1).reshape(count, -1)
        bases.append(whole)

    for wave in range(WAVES):
        for axis in range(2):
            other = 1 - axis
            q = places[other]
            perm = perms[other]
            basis_all = bases[axis]
            group = wave * 2 + axis
            pieces = (slab, [received[wave, axis, distance] for distance in DISTANCES])
            own_tile = (group * SIDE * width + places[axis] * width) // TILE
            tiles = half // TILE
            firsts, seconds = [], []
            for variant in range(2):
                if variant == 0:
                    one, two = (lambda v: v ^ 1), (lambda v: 3 - v)
                else:
                    one, two = (lambda v: 3 - v), (lambda v: v ^ 1)
                partner = one(q)
                where = jnp.stack([two(partner), partner, two(q), q, places[axis], own_tile]).astype(jnp.int32)
                column = variant * tiles
                sent = product_call(
                    first_kernel, "first", where,
                    jax.ShapeDtypeStruct((2 * chunk, half), jnp.bfloat16),
                    pl.BlockSpec((2 * chunk, TILE), lambda t, s: (0, t)),
                    [
                        pl.BlockSpec((chunk, basis_all.shape[1]), lambda t, s: (s[0], 0)),
                        pl.BlockSpec((chunk, basis_all.shape[1]), lambda t, s: (s[1], 0)),
                    ],
                    pieces, (), (), tiles, column, basis_all,
                )
                got = lax.ppermute(sent, "rows", perm(one))
                firsts.append(got)
                sent = product_call(
                    second_kernel, "second", where,
                    jax.ShapeDtypeStruct((chunk, half), jnp.bfloat16),
                    pl.BlockSpec((chunk, TILE), lambda t, s: (0, t)),
                    [pl.BlockSpec((chunk, basis_all.shape[1]), lambda t, s: (s[2], 0))],
                    pieces, (got,), (pl.BlockSpec((chunk, TILE), lambda t, s: (0, t)),), tiles, column, basis_all,
                )
                seconds.append(lax.ppermute(sent, "rows", perm(two)))
            height = chunk // SIDE
            a_tile = lambda t, s: (0, jnp.minimum(t, tiles - 1))
            b_tile = lambda t, s: (0, jnp.maximum(t - tiles, 0))
            a_high = lambda t, s: (1, jnp.minimum(t, tiles - 1))
            b_high = lambda t, s: (1, jnp.maximum(t - tiles, 0))
            out_spec = pl.BlockSpec((height, TILE), lambda t, s: (0, t))
            own, *sends = product_call(
                third_kernel, "third", where,
                [jax.ShapeDtypeStruct((height, width), jnp.float32)]
                + [jax.ShapeDtypeStruct((height, width), jnp.bfloat16)] * 3,
                [out_spec] * 4,
                [pl.BlockSpec((chunk, basis_all.shape[1]), lambda t, s: (s[3], 0))],
                pieces, (firsts[0], seconds[0], firsts[1], seconds[1]),
                tuple(pl.BlockSpec((chunk, TILE), m) for m in (a_high, a_tile, b_high, b_tile)),
                2 * tiles, 0, basis_all,
                (pltpu.VMEM((chunk, TILE), jnp.float32),),
            )
            finals.append(own)
            for distance, send in zip(DISTANCES, sends):
                finals.append(lax.ppermute(send, "rows", perms[axis](lambda v: (v + distance) % SIDE)))

    where = jnp.stack([x, y]).astype(jnp.int32)
    height = count // row_devices
    return pl.pallas_call(
        assemble_kernel,
        grid_spec=pltpu.PrefetchScalarGridSpec(
            num_scalar_prefetch=1,
            grid=(1,),
            in_specs=[pl.BlockSpec((height, width), lambda i, s: (0, 0))] * len(finals),
            out_specs=pl.BlockSpec((height, cols), lambda i, s: (0, 0)),
        ),
        out_shape=jax.ShapeDtypeStruct((height, cols), jnp.float32),
        compiler_params=pltpu.CompilerParams(vmem_limit_bytes=VMEM),
        name="assemble",
    )(where, *finals)


def solution(mesh):
    return jax.shard_map(
        per_device,
        mesh=mesh,
        in_specs=(P("rows", "cols"), P("cols"), P()),
        out_specs=P("rows", "cols"),
        check_vma=False,
    )
```

```python
import functools
import math

import jax
import jax.numpy as jnp
from jax import lax
from jax.experimental import pallas as pl
from jax.experimental.pallas import tpu as pltpu
from jax.sharding import PartitionSpec as P

N = 262144
EPSILON = 1e-06
SIDE = 4
LOW = 2048
SKETCH_BLOCK = 8192
TILE = 1024
EXCHANGE_WAVES = 1
WAVES = 1
DISTANCES = (1, 3, 2)
VMEM = 48 * 1024 * 1024


def x_perm(move):
    return [(y * SIDE + x, y * SIDE + move(x)) for y in range(SIDE) for x in range(SIDE)]


def y_perm(move):
    return [(y * SIDE + x, move(y) * SIDE + x) for y in range(SIDE) for x in range(SIDE)]


def parity_sign(values):
    for shift_by in (16, 8, 4, 2, 1):
        values = jnp.bitwise_xor(values, jnp.right_shift(values, shift_by))
    return (1 - 2 * jnp.bitwise_and(values, 1)).astype(jnp.float32)


def sketch_kernel(first_ref, slab_ref, bits_ref, sampled_ref, out_ref, low_ref, acc_ref):
    step = pl.program_id(0)
    sampled = sampled_ref[...]

    @pl.when(step == 0)
    def _():
        acc_ref[...] = jnp.zeros_like(acc_ref)
        column = lax.broadcasted_iota(jnp.int32, (sampled.shape[0], 128), 1)
        base = parity_sign(jnp.bitwise_and(column, sampled)) * (1.0 / math.sqrt(N))
        for part in range(LOW // 128):
            sign = parity_sign(jnp.bitwise_and(sampled, part * 128))
            low_ref[:, part * 128 : (part + 1) * 128] = (base * sign).astype(jnp.bfloat16)

    total = acc_ref[...]
    for part in range(SKETCH_BLOCK // LOW):
        where = slice(part * LOW, (part + 1) * LOW)
        flip = (1 - 2 * bits_ref[:, where]).astype(jnp.bfloat16)
        signed = slab_ref[:, where] * flip
        term = lax.dot_general(
            low_ref[...], signed, (((1,), (1,)), ((), ())), preferred_element_type=jnp.float32
        )
        high = first_ref[0] + step * SKETCH_BLOCK + part * LOW
        total = total + term * parity_sign(jnp.bitwise_and(sampled, high))
    acc_ref[...] = total

    @pl.when(step == pl.num_programs(0) - 1)
    def _():
        out_ref[...] = acc_ref[...]


def local_sketch(slab, sign_bits, sampled):
    rows, cols = slab.shape
    count = sampled.shape[0]
    first = (lax.axis_index("cols") * cols).astype(jnp.int32).reshape(1)
    return pl.pallas_call(
        sketch_kernel,
        grid_spec=pltpu.PrefetchScalarGridSpec(
            num_scalar_prefetch=1,
            grid=(cols // SKETCH_BLOCK,),
            in_specs=[
                pl.BlockSpec((rows, SKETCH_BLOCK), lambda i, s: (0, i)),
                pl.BlockSpec((1, SKETCH_BLOCK), lambda i, s: (0, i)),
                pl.BlockSpec((count, 1), lambda i, s: (0, 0)),
            ],
            out_specs=pl.BlockSpec((count, rows), lambda i, s: (0, 0)),
            scratch_shapes=[
                pltpu.VMEM((count, LOW), jnp.bfloat16),
                pltpu.VMEM((count, rows), jnp.float32),
            ],
        ),
        out_shape=jax.ShapeDtypeStruct((count, rows), jnp.float32),
        compiler_params=pltpu.CompilerParams(vmem_limit_bytes=VMEM),
        cost_estimate=pl.CostEstimate(
            flops=1, bytes_accessed=1, transcendentals=0
        ),
        name="sketch",
    )(first, slab, sign_bits.reshape(1, cols), sampled.reshape(count, 1))


def assemble_kernel(where_ref, *refs):
    *pieces, out_ref = refs
    scale = 1.0 / math.sqrt(4096)
    base = 0
    for group in range(len(pieces) // SIDE):
        width = pieces[group * SIDE].shape[1]
        place = where_ref[group]
        for k, distance in enumerate((0,) + DISTANCES):
            piece = pieces[group * SIDE + k]
            source = lax.rem(place + SIDE - distance, SIDE)
            column = pl.multiple_of(base + source * width, 128)
            out_ref[:, pl.ds(column, width)] = piece[...].astype(jnp.float32) * scale
        base += SIDE * width


def held_row(row, me, count):
    share = count // 8
    apart = jnp.bitwise_xor(row // share, me)
    step = apart // 2
    slot = jnp.bitwise_xor(step, step // 2) + SIDE * (apart % 2)
    return slot * share + row % share


def product_kernel(axis, where_ref, basis_ref, p0, p1, p2, p3, own, o1, o2, o3, lhs_ref, rhs_ref):
    chunk, depth = own.shape[0], p0.shape[0]
    height = chunk // SIDE
    place = where_ref[1 - axis]

    @pl.when(pl.program_id(0) == 0)
    def _():
        for k, distance in enumerate((0,) + DISTANCES):
            target = lax.rem(place + distance, SIDE)
            for m in range(SIDE):
                row = target * chunk + m * height if axis == 0 else m * chunk + target * height
                row = held_row(row, where_ref[2], basis_ref.shape[0]) if axis else row
                rows = pl.ds(pl.multiple_of(row, height), height)
                to = slice(k * chunk + m * height, k * chunk + (m + 1) * height)
                lhs_ref[to, :] = basis_ref[rows, :]

    for k, piece in enumerate((p0, p1, p2, p3)):
        rhs_ref[k * depth : (k + 1) * depth, :] = piece[...]
    product = jnp.dot(lhs_ref[...], rhs_ref[...], preferred_element_type=jnp.float32)
    for k, out in enumerate((own, o1, o2, o3)):
        out[...] = product[k * chunk : (k + 1) * chunk, :].astype(out.dtype)


def product(axis, where, basis, slab, tile_offset, received, width):
    rows = slab.shape[0]
    count = basis.shape[0]
    chunk = count // SIDE
    block_tiles = slab.shape[1] // (2 * SIDE) // TILE
    depth = SIDE * rows
    return pl.pallas_call(
        functools.partial(product_kernel, axis),
        grid_spec=pltpu.PrefetchScalarGridSpec(
            num_scalar_prefetch=1,
            grid=(width // TILE,),
            in_specs=[
                pl.BlockSpec(basis.shape, lambda t, s: (0, 0)),
                pl.BlockSpec((rows, TILE), lambda t, s: (0, tile_offset + s[axis] * block_tiles + t)),
            ]
            + [pl.BlockSpec((rows, TILE), lambda t, s, first=first: (0, first + t)) for _, first in received],
            out_specs=[pl.BlockSpec((chunk, TILE), lambda t, s: (0, t))] * 4,
            scratch_shapes=[
                pltpu.VMEM((count, depth), jnp.bfloat16),
                pltpu.VMEM((depth, TILE), jnp.bfloat16),
            ],
        ),
        out_shape=[jax.ShapeDtypeStruct((chunk, width), jnp.float32)]
        + [jax.ShapeDtypeStruct((chunk, width), jnp.bfloat16)] * 3,
        compiler_params=pltpu.CompilerParams(vmem_limit_bytes=VMEM),
        cost_estimate=pl.CostEstimate(flops=1, bytes_accessed=1, transcendentals=0),
        name="product",
    )(where, basis, slab, *(piece for piece, _ in received))


def collect_kernel(axis, where_ref, own_ref, g1, g2, g3, *refs):
    *outs, total_ref = refs[-5:]
    total = own_ref[...]
    for got in (g1, g2, g3):
        total = total + got[...].astype(jnp.float32)
    total_ref[...] = total
    height = outs[0].shape[0]
    place = where_ref[axis]
    for out, distance in zip(outs, (0,) + DISTANCES):
        row = lax.rem(place + distance, SIDE) * height
        out[...] = total_ref[pl.ds(pl.multiple_of(row, height), height), :].astype(out.dtype)


def collect(axis, where, own, got, tile_offset, whole_width, earlier):
    chunk, width = own.shape
    height = chunk // SIDE
    return pl.pallas_call(
        functools.partial(collect_kernel, axis),
        grid_spec=pltpu.PrefetchScalarGridSpec(
            num_scalar_prefetch=1,
            grid=(width // TILE,),
            in_specs=[pl.BlockSpec((chunk, TILE), lambda t, s: (0, t))] * 4
            + [pl.BlockSpec(memory_space=pl.ANY)] * len(earlier),
            out_specs=[pl.BlockSpec((height, TILE), lambda t, s: (0, tile_offset + t))] * 4,
            scratch_shapes=[pltpu.VMEM((chunk, TILE), jnp.float32)],
        ),
        out_shape=[jax.ShapeDtypeStruct((height, whole_width), jnp.float32)]
        + [jax.ShapeDtypeStruct((height, whole_width), jnp.bfloat16)] * 3,
        input_output_aliases={5 + k: k for k in range(len(earlier))},
        compiler_params=pltpu.CompilerParams(vmem_limit_bytes=VMEM),
        cost_estimate=pl.CostEstimate(flops=1, bytes_accessed=1, transcendentals=0),
        name="collect",
    )(where, own, *got, *earlier)


PERMS = (x_perm, y_perm)


def shift(value, axis, distance):
    return lax.ppermute(value, "rows", PERMS[axis](lambda q: (q + distance) % SIDE))


def per_device(slab, sign_bits, sampled):
    rows, cols = slab.shape
    count = sampled.shape[0]
    col_devices = lax.axis_size("cols")
    row_devices = lax.axis_size("rows")
    total_rows = rows * row_devices
    share = count // col_devices
    row_index = lax.axis_index("rows")
    places = (row_index % SIDE, row_index // SIDE)
    where = jnp.stack((*places, lax.axis_index("cols"))).astype(jnp.int32)
    width = cols // (2 * SIDE)
    starts = (0, cols // 2)

    def block(source, axis, distance, first=0, size=width):
        start = starts[axis] + (places[axis] + distance) % SIDE * width + first
        return lax.dynamic_slice(source, (0, start), (rows, size))

    x_far, y_far = block(slab, 0, 2), block(slab, 1, 2)
    slab_now, x_far, y_far = lax.optimization_barrier((slab, x_far, y_far))
    x_far, y_far = shift(x_far, 0, 2), shift(y_far, 1, 2)

    partial = local_sketch(slab_now, sign_bits, sampled)
    parts = lax.all_to_all(partial, "cols", 0, 0, tiled=True)
    sketch = jnp.sum(parts.reshape(col_devices, share, rows), axis=0)

    size = width // EXCHANGE_WAVES

    def near_blocks(axis):
        return [[block(slab_now, axis, d, w * size, size) for d in (1, 3)] for w in range(EXCHANGE_WAVES)]

    def send_near(blocks, axis):
        return [[shift(part, axis, d) for part, d in zip(pair, (1, 3))] for pair in blocks]

    x_sketch = [sketch] + [shift(sketch, 0, distance) for distance in DISTANCES]
    x_near, x_sketch, x_far = lax.optimization_barrier((near_blocks(0), x_sketch, x_far))
    x_near = send_near(x_near, 0)
    x_squares = sum(jnp.sum(part * part, axis=1, keepdims=True) for part in x_sketch)
    sent = jnp.concatenate([sketch, jnp.broadcast_to(x_squares, (share, 128))], axis=1)
    y_sketch = [sent] + [shift(sent, 1, distance) for distance in DISTANCES]
    y_near, y_sketch, y_far = lax.optimization_barrier((near_blocks(1), y_sketch, y_far))
    y_near = send_near(y_near, 1)
    squares = sum(part[:, rows : rows + 1] for part in y_sketch)
    scale = lax.rsqrt(squares / total_rows + EPSILON)

    bases = []
    for sketches in (x_sketch, y_sketch):
        joined = jnp.concatenate([(part[:, :rows] * scale).astype(jnp.bfloat16) for part in sketches], axis=1)
        bases.append(joined)
    bases[0] = lax.all_to_all(jnp.tile(bases[0], (col_devices, 1)), "cols", 0, 0, tiled=True)
    for mask in (2, 6, 1):
        other = lax.ppermute(bases[1], "cols", [(k, k ^ mask) for k in range(col_devices)])
        bases[1] = jnp.concatenate([bases[1], other], axis=0)

    far, near = (x_far, y_far), (x_near, y_near)
    height = count // row_devices
    wave_width = width // WAVES
    wave_tiles = wave_width // TILE
    collected = [(), ()]
    for wave in range(WAVES):
        terms = []
        for axis in range(2):
            first = wave * wave_tiles
            if EXCHANGE_WAVES > 1:
                one, three = ((part, 0) for part in near[axis][wave])
            else:
                one, three = ((part, first) for part in near[axis][0])
            offset = starts[axis] // TILE + first
            own, *sends = product(axis, where, bases[axis], slab, offset, (one, three, (far[axis], first)), wave_width)
            order = (2, 0, 1)
            got = {k: shift(sends[k], 1 - axis, DISTANCES[k]) for k in order}
            terms.append((own, [got[k] for k in range(3)]))
        for axis in range(2):
            own, got = terms[axis]
            collected[axis] = collect(axis, where, own, got, wave * wave_tiles, width, collected[axis])
    pieces = []
    for axis in range(2):
        own, *sends = collected[axis]
        pieces += [own] + [shift(send, axis, distance) for send, distance in zip(sends, DISTANCES)]
    return pl.pallas_call(
        assemble_kernel,
        grid_spec=pltpu.PrefetchScalarGridSpec(
            num_scalar_prefetch=1,
            grid=(1,),
            in_specs=[pl.BlockSpec(piece.shape, lambda i, s: (0, 0)) for piece in pieces],
            out_specs=pl.BlockSpec((height, cols), lambda i, s: (0, 0)),
        ),
        out_shape=jax.ShapeDtypeStruct((height, cols), jnp.float32),
        compiler_params=pltpu.CompilerParams(vmem_limit_bytes=VMEM),
        name="assemble",
    )(where, *pieces)


def solution(mesh):
    return jax.shard_map(
        per_device,
        mesh=mesh,
        in_specs=(P("rows", "cols"), P("cols"), P()),
        out_specs=P("rows", "cols"),
        check_vma=False,
    )
```

```python
import functools
import math

import jax
import jax.numpy as jnp
from jax import lax
from jax.experimental import pallas as pl
from jax.experimental.pallas import tpu as pltpu
from jax.sharding import PartitionSpec as P

N = 262144
EPSILON = 1e-06
SIDE = 4
LOW = 2048
SKETCH_BLOCK = 8192
TILE = 1024
DISTANCES = (1, 3, 2)
VMEM = 48 * 1024 * 1024


def x_perm(move):
    return [(y * SIDE + x, y * SIDE + move(x)) for y in range(SIDE) for x in range(SIDE)]


def y_perm(move):
    return [(y * SIDE + x, move(y) * SIDE + x) for y in range(SIDE) for x in range(SIDE)]


def parity_sign(values):
    for shift_by in (16, 8, 4, 2, 1):
        values = jnp.bitwise_xor(values, jnp.right_shift(values, shift_by))
    return (1 - 2 * jnp.bitwise_and(values, 1)).astype(jnp.float32)


def sketch_kernel(first_ref, slab_ref, bits_ref, sampled_ref, out_ref, low_ref, acc_ref):
    step = pl.program_id(0)
    sampled = sampled_ref[...]

    @pl.when(step == 0)
    def _():
        acc_ref[...] = jnp.zeros_like(acc_ref)
        column = lax.broadcasted_iota(jnp.int32, (sampled.shape[0], 128), 1)
        base = parity_sign(jnp.bitwise_and(column, sampled)) * (1.0 / math.sqrt(N))
        for part in range(LOW // 128):
            sign = parity_sign(jnp.bitwise_and(sampled, part * 128))
            low_ref[:, part * 128 : (part + 1) * 128] = (base * sign).astype(jnp.bfloat16)

    total = acc_ref[...]
    for part in range(SKETCH_BLOCK // LOW):
        where = slice(part * LOW, (part + 1) * LOW)
        flip = (1 - 2 * bits_ref[:, where]).astype(jnp.bfloat16)
        signed = slab_ref[:, where] * flip
        term = lax.dot_general(
            low_ref[...], signed, (((1,), (1,)), ((), ())), preferred_element_type=jnp.float32
        )
        high = first_ref[0] + step * SKETCH_BLOCK + part * LOW
        total = total + term * parity_sign(jnp.bitwise_and(sampled, high))
    acc_ref[...] = total

    @pl.when(step == pl.num_programs(0) - 1)
    def _():
        out_ref[...] = acc_ref[...]


def local_sketch(slab, sign_bits, sampled):
    rows, cols = slab.shape
    count = sampled.shape[0]
    first = (lax.axis_index("cols") * cols).astype(jnp.int32).reshape(1)
    return pl.pallas_call(
        sketch_kernel,
        grid_spec=pltpu.PrefetchScalarGridSpec(
            num_scalar_prefetch=1,
            grid=(cols // SKETCH_BLOCK,),
            in_specs=[
                pl.BlockSpec((rows, SKETCH_BLOCK), lambda i, s: (0, i)),
                pl.BlockSpec((1, SKETCH_BLOCK), lambda i, s: (0, i)),
                pl.BlockSpec((count, 1), lambda i, s: (0, 0)),
            ],
            out_specs=pl.BlockSpec((count, rows), lambda i, s: (0, 0)),
            scratch_shapes=[
                pltpu.VMEM((count, LOW), jnp.bfloat16),
                pltpu.VMEM((count, rows), jnp.float32),
            ],
        ),
        out_shape=jax.ShapeDtypeStruct((count, rows), jnp.float32),
        compiler_params=pltpu.CompilerParams(vmem_limit_bytes=VMEM),
        cost_estimate=pl.CostEstimate(
            flops=1, bytes_accessed=1, transcendentals=0
        ),
        name="sketch",
    )(first, slab, sign_bits.reshape(1, cols), sampled.reshape(count, 1))


def assemble_kernel(axis, where_ref, own, g1, g2, g3, one, three, far, *refs):
    out_ref = refs[-1]
    scale = 1.0 / math.sqrt(4096)
    width = own.shape[1]
    total = own[...]
    for got in (g1, g2, g3):
        total = total + got[...].astype(jnp.float32)
    pieces = (total, one[...], three[...], far[...])
    for piece, distance in zip(pieces, (0,) + DISTANCES):
        source = lax.rem(where_ref[axis] + SIDE - distance, SIDE)
        column = pl.multiple_of(source * width, width)
        out_ref[:, pl.ds(column, width)] = piece.astype(jnp.float32) * scale


def assemble(axis, where, own, got, pieces, earlier):
    height, width = pieces[0].shape
    return pl.pallas_call(
        functools.partial(assemble_kernel, axis),
        grid_spec=pltpu.PrefetchScalarGridSpec(
            num_scalar_prefetch=1,
            grid=(1,),
            in_specs=[pl.BlockSpec((height, width), lambda i, s: (SIDE - 1, 0))] * SIDE
            + [pl.BlockSpec((height, width), lambda i, s: (0, 0))] * 3
            + [pl.BlockSpec(memory_space=pl.ANY)] * len(earlier),
            out_specs=pl.BlockSpec((height, SIDE * width), lambda i, s: (0, axis)),
        ),
        out_shape=jax.ShapeDtypeStruct((height, 2 * SIDE * width), jnp.float32),
        input_output_aliases={8 + k: k for k in range(len(earlier))},
        compiler_params=pltpu.CompilerParams(vmem_limit_bytes=VMEM),
        cost_estimate=pl.CostEstimate(flops=1, bytes_accessed=1, transcendentals=0),
        name="assemble",
    )(where, own, *got, *pieces, *earlier)


def held_row(row, me, count):
    share = count // 8
    apart = jnp.bitwise_xor(row // share, me)
    step = apart // 2
    slot = jnp.bitwise_xor(step, step // 2) + SIDE * (apart % 2)
    return slot * share + row % share


def product_kernel(axis, distances, where_ref, basis_ref, p0, p1, p2, p3, *refs):
    *outs, lhs_ref, rhs_ref = refs
    chunk, depth = outs[0].shape[0], p0.shape[0]
    height = chunk // SIDE
    place = where_ref[1 - axis]

    @pl.when(pl.program_id(0) == 0)
    def _():
        for k, distance in enumerate(distances):
            target = lax.rem(place + distance, SIDE)
            for m, step in enumerate(DISTANCES + (0,)):
                other = lax.rem(where_ref[axis] + step, SIDE)
                row = target * chunk + other * height if axis == 0 else other * chunk + target * height
                row = held_row(row, where_ref[2], basis_ref.shape[0]) if axis else row
                rows = pl.ds(pl.multiple_of(row, height), height)
                to = slice(k * chunk + m * height, k * chunk + (m + 1) * height)
                lhs_ref[to, :] = basis_ref[rows, :]

    for k, piece in enumerate((p0, p1, p2, p3)):
        rhs_ref[k * depth : (k + 1) * depth, :] = piece[...]
    product = jnp.dot(lhs_ref[...], rhs_ref[...], preferred_element_type=jnp.float32)
    for k, out in enumerate(outs):
        out[...] = product[k * chunk : (k + 1) * chunk, :].astype(out.dtype)


def product(axis, distances, where, basis, slab, received):
    rows, width = received[0].shape
    count = basis.shape[0]
    chunk = count // SIDE
    tiles = width // TILE
    depth = SIDE * rows
    height = chunk * len(distances)
    return pl.pallas_call(
        functools.partial(product_kernel, axis, distances),
        grid_spec=pltpu.PrefetchScalarGridSpec(
            num_scalar_prefetch=1,
            grid=(tiles,),
            in_specs=[
                pl.BlockSpec(basis.shape, lambda t, s: (0, 0)),
                pl.BlockSpec((rows, TILE), lambda t, s: (0, (axis * SIDE + s[axis]) * tiles + t)),
            ]
            + [pl.BlockSpec((rows, TILE), lambda t, s: (0, t))] * 3,
            out_specs=[pl.BlockSpec((chunk, TILE), lambda t, s: (0, t))] * len(distances),
            scratch_shapes=[
                pltpu.VMEM((height, depth), jnp.bfloat16),
                pltpu.VMEM((depth, TILE), jnp.bfloat16),
            ],
        ),
        out_shape=[
            jax.ShapeDtypeStruct((chunk, width), jnp.bfloat16 if distance else jnp.float32) for distance in distances
        ],
        compiler_params=pltpu.CompilerParams(vmem_limit_bytes=VMEM),
        cost_estimate=pl.CostEstimate(flops=1, bytes_accessed=1, transcendentals=0),
        name="product",
    )(where, basis, slab, *received)


def collect_kernel(own_ref, g1, g2, g3, *outs):
    total = own_ref[...]
    for got in (g1, g2, g3):
        total = total + got[...].astype(jnp.float32)
    height = outs[0].shape[0]
    for k, out in enumerate(outs):
        out[...] = total[k * height : (k + 1) * height, :].astype(out.dtype)


def collect(own, got, first, blocks):
    chunk, width = own.shape
    height = chunk // SIDE
    rows = height * blocks
    return pl.pallas_call(
        collect_kernel,
        grid=(width // TILE,),
        in_specs=[pl.BlockSpec((rows, TILE), lambda t: (first // blocks, t))] * 4,
        out_specs=[pl.BlockSpec((height, TILE), lambda t: (0, t))] * blocks,
        out_shape=[jax.ShapeDtypeStruct((height, width), jnp.bfloat16)] * blocks,
        compiler_params=pltpu.CompilerParams(vmem_limit_bytes=VMEM),
        cost_estimate=pl.CostEstimate(flops=1, bytes_accessed=1, transcendentals=0),
        name="collect",
    )(own, *got)


PERMS = (x_perm, y_perm)


def shift(value, axis, distance):
    return lax.ppermute(value, "rows", PERMS[axis](lambda q: (q + distance) % SIDE))


def per_device(slab, sign_bits, sampled):
    rows, cols = slab.shape
    count = sampled.shape[0]
    col_devices = lax.axis_size("cols")
    row_devices = lax.axis_size("rows")
    total_rows = rows * row_devices
    share = count // col_devices
    row_index = lax.axis_index("rows")
    places = (row_index % SIDE, row_index // SIDE)
    where = jnp.stack((*places, lax.axis_index("cols"))).astype(jnp.int32)
    width = cols // (2 * SIDE)
    starts = (0, cols // 2)

    def block(source, axis, distance, first=0, size=width):
        start = starts[axis] + (places[axis] + distance) % SIDE * width + first
        return lax.dynamic_slice(source, (0, start), (rows, size))

    slab_x, x_far = lax.optimization_barrier((slab, block(slab, 0, 2)))
    x_far = shift(x_far, 0, 2)
    slab_now, y_far = lax.optimization_barrier((slab_x, block(slab_x, 1, 2)))
    y_far = shift(y_far, 1, 2)

    partial = local_sketch(slab_now, sign_bits, sampled)
    parts = lax.all_to_all(partial, "cols", 0, 0, tiled=True)
    sketch = jnp.sum(parts.reshape(col_devices, share, rows), axis=0)

    def near_blocks(axis):
        return [block(slab_now, axis, distance) for distance in (1, 3)]

    def send_near(blocks, axis):
        return [shift(part, axis, distance) for part, distance in zip(blocks, (1, 3))]

    x_sketch = [sketch] + [shift(sketch, 0, distance) for distance in DISTANCES]
    x_near, x_sketch, x_far = lax.optimization_barrier((near_blocks(0), x_sketch, x_far))
    x_near = send_near(x_near, 0)
    x_squares = sum(jnp.sum(part * part, axis=1, keepdims=True) for part in x_sketch)
    sent = jnp.concatenate([sketch, jnp.broadcast_to(x_squares, (share, 128))], axis=1)
    y_sketch = [sent] + [shift(sent, 1, distance) for distance in DISTANCES]
    y_near, y_sketch, y_far = lax.optimization_barrier((near_blocks(1), y_sketch, y_far))
    y_near = send_near(y_near, 1)
    squares = sum(part[:, rows : rows + 1] for part in y_sketch)
    scale = lax.rsqrt(squares / total_rows + EPSILON)

    bases = []
    for sketches in (x_sketch, y_sketch):
        joined = jnp.concatenate([(part[:, :rows] * scale).astype(jnp.bfloat16) for part in sketches], axis=1)
        bases.append(joined)
    bases[0] = lax.all_to_all(jnp.tile(bases[0], (col_devices, 1)), "cols", 0, 0, tiled=True)
    for mask in (2, 6, 1):
        other = lax.ppermute(bases[1], "cols", [(k, k ^ mask) for k in range(col_devices)])
        bases[1] = jnp.concatenate([bases[1], other], axis=0)

    x_received, y_received = (*x_near, x_far), (*y_near, y_far)
    terms = [
        product(axis, (0,) + DISTANCES, where, bases[axis], slab, received)
        for axis, received in enumerate((x_received, y_received))
    ]
    out = ()
    for axis in range(2):
        own, *sends = terms[axis]
        got = [shift(send, 1 - axis, distance) for send, distance in zip(sends, DISTANCES)]
        (far,) = collect(own, got, 2, 1)
        far = shift(far, axis, 2)
        near = collect(own, got, 0, 2)
        near = [shift(part, axis, distance) for part, distance in zip(near, (1, 3))]
        out = (assemble(axis, where, own, got, (*near, far), out),)
    return out[0]


def solution(mesh):
    return jax.shard_map(
        per_device,
        mesh=mesh,
        in_specs=(P("rows", "cols"), P("cols"), P()),
        out_specs=P("rows", "cols"),
        check_vma=False,
    )
```

```python
import functools
import math

import jax
import jax.numpy as jnp
from jax import lax
from jax.experimental import pallas as pl
from jax.experimental.pallas import tpu as pltpu
from jax.sharding import PartitionSpec as P

N = 262144
EPSILON = 1e-06
SIDE = 4
LOW = 2048
SKETCH_BLOCK = 8192
TILE = 1024
DISTANCES = (1, 3, 2)
VMEM = 48 * 1024 * 1024


def x_perm(move):
    return [(y * SIDE + x, y * SIDE + move(x)) for y in range(SIDE) for x in range(SIDE)]


def y_perm(move):
    return [(y * SIDE + x, move(y) * SIDE + x) for y in range(SIDE) for x in range(SIDE)]


def parity_sign(values):
    for shift_by in (16, 8, 4, 2, 1):
        values = jnp.bitwise_xor(values, jnp.right_shift(values, shift_by))
    return (1 - 2 * jnp.bitwise_and(values, 1)).astype(jnp.float32)


def sketch_kernel(first_ref, slab_ref, bits_ref, sampled_ref, out_ref, low_ref, acc_ref):
    step = pl.program_id(0)
    sampled = sampled_ref[...]

    @pl.when(step == 0)
    def _():
        acc_ref[...] = jnp.zeros_like(acc_ref)
        column = lax.broadcasted_iota(jnp.int32, (sampled.shape[0], 128), 1)
        base = parity_sign(jnp.bitwise_and(column, sampled)) * (1.0 / math.sqrt(N))
        for part in range(LOW // 128):
            sign = parity_sign(jnp.bitwise_and(sampled, part * 128))
            low_ref[:, part * 128 : (part + 1) * 128] = (base * sign).astype(jnp.bfloat16)

    total = acc_ref[...]
    for part in range(SKETCH_BLOCK // LOW):
        where = slice(part * LOW, (part + 1) * LOW)
        flip = (1 - 2 * bits_ref[:, where]).astype(jnp.bfloat16)
        signed = slab_ref[:, where] * flip
        term = lax.dot_general(
            low_ref[...], signed, (((1,), (1,)), ((), ())), preferred_element_type=jnp.float32
        )
        high = first_ref[0] + step * SKETCH_BLOCK + part * LOW
        total = total + term * parity_sign(jnp.bitwise_and(sampled, high))
    acc_ref[...] = total

    @pl.when(step == pl.num_programs(0) - 1)
    def _():
        out_ref[...] = acc_ref[...]


def local_sketch(slab, sign_bits, sampled):
    rows, cols = slab.shape
    count = sampled.shape[0]
    first = (lax.axis_index("cols") * cols).astype(jnp.int32).reshape(1)
    return pl.pallas_call(
        sketch_kernel,
        grid_spec=pltpu.PrefetchScalarGridSpec(
            num_scalar_prefetch=1,
            grid=(cols // SKETCH_BLOCK,),
            in_specs=[
                pl.BlockSpec((rows, SKETCH_BLOCK), lambda i, s: (0, i)),
                pl.BlockSpec((1, SKETCH_BLOCK), lambda i, s: (0, i)),
                pl.BlockSpec((count, 1), lambda i, s: (0, 0)),
            ],
            out_specs=pl.BlockSpec((count, rows), lambda i, s: (0, 0)),
            scratch_shapes=[
                pltpu.VMEM((count, LOW), jnp.bfloat16),
                pltpu.VMEM((count, rows), jnp.float32),
            ],
        ),
        out_shape=jax.ShapeDtypeStruct((count, rows), jnp.float32),
        compiler_params=pltpu.CompilerParams(vmem_limit_bytes=VMEM),
        cost_estimate=pl.CostEstimate(
            flops=1, bytes_accessed=1, transcendentals=0
        ),
        name="sketch",
    )(first, slab, sign_bits.reshape(1, cols), sampled.reshape(count, 1))


def assemble_kernel(axis, where_ref, own, g1, g2, g3, one, three, far, *refs):
    out_ref = refs[-1]
    scale = 1.0 / math.sqrt(4096)
    width = own.shape[1]
    total = own[...]
    for got in (g1, g2, g3):
        total = total + got[...].astype(jnp.float32)
    pieces = (total, one[...], three[...], far[...])
    for piece, distance in zip(pieces, (0,) + DISTANCES):
        source = lax.rem(where_ref[axis] + SIDE - distance, SIDE)
        column = pl.multiple_of(source * width, width)
        out_ref[:, pl.ds(column, width)] = piece.astype(jnp.float32) * scale


def assemble(axis, where, own, got, pieces, earlier):
    height, width = pieces[0].shape
    return pl.pallas_call(
        functools.partial(assemble_kernel, axis),
        grid_spec=pltpu.PrefetchScalarGridSpec(
            num_scalar_prefetch=1,
            grid=(1,),
            in_specs=[pl.BlockSpec((height, width), lambda i, s: (SIDE - 1, 0))] * SIDE
            + [pl.BlockSpec((height, width), lambda i, s: (0, 0))] * 3
            + [pl.BlockSpec(memory_space=pl.ANY)] * len(earlier),
            out_specs=pl.BlockSpec((height, SIDE * width), lambda i, s: (0, axis)),
        ),
        out_shape=jax.ShapeDtypeStruct((height, 2 * SIDE * width), jnp.float32),
        input_output_aliases={8 + k: k for k in range(len(earlier))},
        compiler_params=pltpu.CompilerParams(vmem_limit_bytes=VMEM),
        cost_estimate=pl.CostEstimate(flops=1, bytes_accessed=1, transcendentals=0),
        name="assemble",
    )(where, own, *got, *pieces, *earlier)


def held_row(row, me, count):
    share = count // 8
    apart = jnp.bitwise_xor(row // share, me)
    step = apart // 2
    slot = jnp.bitwise_xor(step, step // 2) + SIDE * (apart % 2)
    return slot * share + row % share


def product_kernel(axis, distances, where_ref, basis_ref, p0, p1, p2, p3, *refs):
    *outs, lhs_ref, rhs_ref = refs
    chunk, depth = outs[0].shape[0], p0.shape[0]
    height = chunk // SIDE
    place = where_ref[1 - axis]

    @pl.when(pl.program_id(0) == 0)
    def _():
        for k, distance in enumerate(distances):
            target = lax.rem(place + distance, SIDE)
            for m, step in enumerate(DISTANCES + (0,)):
                other = lax.rem(where_ref[axis] + step, SIDE)
                row = target * chunk + other * height if axis == 0 else other * chunk + target * height
                row = held_row(row, where_ref[2], basis_ref.shape[0]) if axis else row
                rows = pl.ds(pl.multiple_of(row, height), height)
                to = slice(k * chunk + m * height, k * chunk + (m + 1) * height)
                lhs_ref[to, :] = basis_ref[rows, :]

    for k, piece in enumerate((p0, p1, p2, p3)):
        rhs_ref[k * depth : (k + 1) * depth, :] = piece[...]
    product = jnp.dot(lhs_ref[...], rhs_ref[...], preferred_element_type=jnp.float32)
    for k, out in enumerate(outs):
        out[...] = product[k * chunk : (k + 1) * chunk, :].astype(out.dtype)


def product(axis, distances, where, basis, slab, received):
    rows, width = received[0].shape
    count = basis.shape[0]
    chunk = count // SIDE
    tiles = width // TILE
    depth = SIDE * rows
    height = chunk * len(distances)
    return pl.pallas_call(
        functools.partial(product_kernel, axis, distances),
        grid_spec=pltpu.PrefetchScalarGridSpec(
            num_scalar_prefetch=1,
            grid=(tiles,),
            in_specs=[
                pl.BlockSpec(basis.shape, lambda t, s: (0, 0)),
                pl.BlockSpec((rows, TILE), lambda t, s: (0, (axis * SIDE + s[axis]) * tiles + t)),
            ]
            + [pl.BlockSpec((rows, TILE), lambda t, s: (0, t))] * 3,
            out_specs=[pl.BlockSpec((chunk, TILE), lambda t, s: (0, t))] * len(distances),
            scratch_shapes=[
                pltpu.VMEM((height, depth), jnp.bfloat16),
                pltpu.VMEM((depth, TILE), jnp.bfloat16),
            ],
        ),
        out_shape=[
            jax.ShapeDtypeStruct((chunk, width), jnp.bfloat16 if distance else jnp.float32) for distance in distances
        ],
        compiler_params=pltpu.CompilerParams(vmem_limit_bytes=VMEM),
        cost_estimate=pl.CostEstimate(flops=1, bytes_accessed=1, transcendentals=0),
        name="product",
    )(where, basis, slab, *received)


def collect_kernel(own_ref, g1, g2, g3, *outs):
    total = own_ref[...]
    for got in (g1, g2, g3):
        total = total + got[...].astype(jnp.float32)
    height = outs[0].shape[0]
    for k, out in enumerate(outs):
        out[...] = total[k * height : (k + 1) * height, :].astype(out.dtype)


def collect(own, got, first, blocks):
    chunk, width = own.shape
    height = chunk // SIDE
    rows = height * blocks
    return pl.pallas_call(
        collect_kernel,
        grid=(width // TILE,),
        in_specs=[pl.BlockSpec((rows, TILE), lambda t: (first // blocks, t))] * 4,
        out_specs=[pl.BlockSpec((height, TILE), lambda t: (0, t))] * blocks,
        out_shape=[jax.ShapeDtypeStruct((height, width), jnp.bfloat16)] * blocks,
        compiler_params=pltpu.CompilerParams(vmem_limit_bytes=VMEM),
        cost_estimate=pl.CostEstimate(flops=1, bytes_accessed=1, transcendentals=0),
        name="collect",
    )(own, *got)


PERMS = (x_perm, y_perm)


def shift(value, axis, distance):
    return lax.ppermute(value, "rows", PERMS[axis](lambda q: (q + distance) % SIDE))


def per_device(slab, sign_bits, sampled):
    rows, cols = slab.shape
    count = sampled.shape[0]
    col_devices = lax.axis_size("cols")
    row_devices = lax.axis_size("rows")
    total_rows = rows * row_devices
    share = count // col_devices
    row_index = lax.axis_index("rows")
    places = (row_index % SIDE, row_index // SIDE)
    where = jnp.stack((*places, lax.axis_index("cols"))).astype(jnp.int32)
    width = cols // (2 * SIDE)
    starts = (0, cols // 2)

    def block(source, axis, distance, first=0, size=width):
        start = starts[axis] + (places[axis] + distance) % SIDE * width + first
        return lax.dynamic_slice(source, (0, start), (rows, size))

    slab_first, x_first = lax.optimization_barrier((slab, block(slab, 0, 2, 0, TILE)))
    slab_x, x_rest = lax.optimization_barrier((slab_first, block(slab_first, 0, 2, TILE, width - TILE)))
    x_far = [shift(x_first, 0, 2), shift(x_rest, 0, 2)]
    slab_now, y_far = lax.optimization_barrier((slab_x, block(slab_x, 1, 2)))
    y_far = shift(y_far, 1, 2)

    partial = local_sketch(slab_now, sign_bits, sampled)
    parts = lax.all_to_all(partial, "cols", 0, 0, tiled=True)
    sketch = jnp.sum(parts.reshape(col_devices, share, rows), axis=0)

    def near_blocks(axis):
        return [block(slab_now, axis, distance) for distance in (1, 3)]

    def send_near(blocks, axis):
        return [shift(part, axis, distance) for part, distance in zip(blocks, (1, 3))]

    x_sketch = [sketch] + [shift(sketch, 0, distance) for distance in DISTANCES]
    x_near, x_sketch, x_far = lax.optimization_barrier((near_blocks(0), x_sketch, x_far))
    x_near = send_near(x_near, 0)
    x_squares = sum(jnp.sum(part * part, axis=1, keepdims=True) for part in x_sketch)
    sent = jnp.concatenate([sketch, jnp.broadcast_to(x_squares, (share, 128))], axis=1)
    y_sketch = [sent] + [shift(sent, 1, distance) for distance in DISTANCES]
    y_near, y_sketch, y_far = lax.optimization_barrier((near_blocks(1), y_sketch, y_far))
    y_near = send_near(y_near, 1)
    squares = sum(part[:, rows : rows + 1] for part in y_sketch)
    scale = lax.rsqrt(squares / total_rows + EPSILON)

    bases = []
    for sketches in (x_sketch, y_sketch):
        joined = jnp.concatenate([(part[:, :rows] * scale).astype(jnp.bfloat16) for part in sketches], axis=1)
        bases.append(joined)
    x_far, bases[0] = lax.optimization_barrier((jnp.concatenate(x_far, axis=1), bases[0]))
    bases[0] = lax.all_to_all(jnp.tile(bases[0], (col_devices, 1)), "cols", 0, 0, tiled=True)
    for mask in (2, 6, 1):
        other = lax.ppermute(bases[1], "cols", [(k, k ^ mask) for k in range(col_devices)])
        bases[1] = jnp.concatenate([bases[1], other], axis=0)

    x_received, y_received = (*x_near, x_far), (*y_near, y_far)
    terms = [
        product(axis, (0,) + DISTANCES, where, bases[axis], slab, received)
        for axis, received in enumerate((x_received, y_received))
    ]
    out = ()
    for axis in range(2):
        own, *sends = terms[axis]
        got = [shift(send, 1 - axis, distance) for send, distance in zip(sends, DISTANCES)]
        (far,) = collect(own, got, 2, 1)
        far = shift(far, axis, 2)
        near = collect(own, got, 0, 2)
        near = [shift(part, axis, distance) for part, distance in zip(near, (1, 3))]
        out = (assemble(axis, where, own, got, (*near, far), out),)
    return out[0]


def solution(mesh):
    return jax.shard_map(
        per_device,
        mesh=mesh,
        in_specs=(P("rows", "cols"), P("cols"), P()),
        out_specs=P("rows", "cols"),
        check_vma=False,
    )
```

```python
import functools
import math

import jax
import jax.numpy as jnp
from jax import lax
from jax.experimental import pallas as pl
from jax.experimental.pallas import tpu as pltpu
from jax.sharding import PartitionSpec as P

N = 262144
EPSILON = 1e-06
SIDE = 4
LOW = 2048
SKETCH_BLOCK = 8192
TILE = 1024
DISTANCES = (1, 3, 2)
VMEM = 48 * 1024 * 1024


def x_perm(move):
    return [(y * SIDE + x, y * SIDE + move(x)) for y in range(SIDE) for x in range(SIDE)]


def y_perm(move):
    return [(y * SIDE + x, move(y) * SIDE + x) for y in range(SIDE) for x in range(SIDE)]


def parity_sign(values):
    for shift_by in (16, 8, 4, 2, 1):
        values = jnp.bitwise_xor(values, jnp.right_shift(values, shift_by))
    return (1 - 2 * jnp.bitwise_and(values, 1)).astype(jnp.float32)


def sketch_kernel(first_ref, slab_ref, bits_ref, sampled_ref, out_ref, low_ref, acc_ref):
    step = pl.program_id(0)
    sampled = sampled_ref[...]

    @pl.when(step == 0)
    def _():
        acc_ref[...] = jnp.zeros_like(acc_ref)
        column = lax.broadcasted_iota(jnp.int32, (sampled.shape[0], 128), 1)
        base = parity_sign(jnp.bitwise_and(column, sampled)) * (1.0 / math.sqrt(N))
        for part in range(LOW // 128):
            sign = parity_sign(jnp.bitwise_and(sampled, part * 128))
            low_ref[:, part * 128 : (part + 1) * 128] = (base * sign).astype(jnp.bfloat16)

    total = acc_ref[...]
    for part in range(SKETCH_BLOCK // LOW):
        where = slice(part * LOW, (part + 1) * LOW)
        flip = (1 - 2 * bits_ref[:, where]).astype(jnp.bfloat16)
        signed = slab_ref[:, where] * flip
        term = lax.dot_general(
            low_ref[...], signed, (((1,), (1,)), ((), ())), preferred_element_type=jnp.float32
        )
        high = first_ref[0] + step * SKETCH_BLOCK + part * LOW
        total = total + term * parity_sign(jnp.bitwise_and(sampled, high))
    acc_ref[...] = total

    @pl.when(step == pl.num_programs(0) - 1)
    def _():
        out_ref[...] = acc_ref[...]


def local_sketch(slab, sign_bits, sampled):
    rows, cols = slab.shape
    count = sampled.shape[0]
    first = (lax.axis_index("cols") * cols).astype(jnp.int32).reshape(1)
    return pl.pallas_call(
        sketch_kernel,
        grid_spec=pltpu.PrefetchScalarGridSpec(
            num_scalar_prefetch=1,
            grid=(cols // SKETCH_BLOCK,),
            in_specs=[
                pl.BlockSpec((rows, SKETCH_BLOCK), lambda i, s: (0, i)),
                pl.BlockSpec((1, SKETCH_BLOCK), lambda i, s: (0, i)),
                pl.BlockSpec((count, 1), lambda i, s: (0, 0)),
            ],
            out_specs=pl.BlockSpec((count, rows), lambda i, s: (0, 0)),
            scratch_shapes=[
                pltpu.VMEM((count, LOW), jnp.bfloat16),
                pltpu.VMEM((count, rows), jnp.float32),
            ],
        ),
        out_shape=jax.ShapeDtypeStruct((count, rows), jnp.float32),
        compiler_params=pltpu.CompilerParams(vmem_limit_bytes=VMEM),
        cost_estimate=pl.CostEstimate(
            flops=1, bytes_accessed=1, transcendentals=0
        ),
        name="sketch",
    )(first, slab, sign_bits.reshape(1, cols), sampled.reshape(count, 1))


def assemble_kernel(axis, where_ref, own, g1, g2, g3, one, three, far, *refs):
    out_ref = refs[-1]
    scale = 1.0 / math.sqrt(4096)
    width = own.shape[1]
    total = own[...]
    for got in (g1, g2, g3):
        total = total + got[...].astype(jnp.float32)
    pieces = (total, one[...], three[...], far[...])
    for piece, distance in zip(pieces, (0,) + DISTANCES):
        source = lax.rem(where_ref[axis] + SIDE - distance, SIDE)
        column = pl.multiple_of(source * width, width)
        out_ref[:, pl.ds(column, width)] = piece.astype(jnp.float32) * scale


def assemble(axis, where, own, got, pieces, earlier):
    height, width = pieces[0].shape
    return pl.pallas_call(
        functools.partial(assemble_kernel, axis),
        grid_spec=pltpu.PrefetchScalarGridSpec(
            num_scalar_prefetch=1,
            grid=(1,),
            in_specs=[pl.BlockSpec((height, width), lambda i, s: (SIDE - 1, 0))] * SIDE
            + [pl.BlockSpec((height, width), lambda i, s: (0, 0))] * 3
            + [pl.BlockSpec(memory_space=pl.ANY)] * len(earlier),
            out_specs=pl.BlockSpec((height, SIDE * width), lambda i, s: (0, axis)),
        ),
        out_shape=jax.ShapeDtypeStruct((height, 2 * SIDE * width), jnp.float32),
        input_output_aliases={8 + k: k for k in range(len(earlier))},
        compiler_params=pltpu.CompilerParams(vmem_limit_bytes=VMEM),
        cost_estimate=pl.CostEstimate(flops=1, bytes_accessed=1, transcendentals=0),
        name="assemble",
    )(where, own, *got, *pieces, *earlier)


def held_row(row, me, count):
    share = count // 8
    apart = jnp.bitwise_xor(row // share, me)
    step = apart // 2
    slot = jnp.bitwise_xor(step, step // 2) + SIDE * (apart % 2)
    return slot * share + row % share


def product_kernel(axis, distances, where_ref, basis_ref, p0, p1, p2, p3, *refs):
    *outs, lhs_ref, rhs_ref = refs
    chunk, depth = outs[0].shape[0], p0.shape[0]
    height = chunk // SIDE
    place = where_ref[1 - axis]

    @pl.when(pl.program_id(0) == 0)
    def _():
        for k, distance in enumerate(distances):
            target = lax.rem(place + distance, SIDE)
            for m, step in enumerate(DISTANCES + (0,)):
                other = lax.rem(where_ref[axis] + step, SIDE)
                row = target * chunk + other * height if axis == 0 else other * chunk + target * height
                row = held_row(row, where_ref[2], basis_ref.shape[0]) if axis else row
                rows = pl.ds(pl.multiple_of(row, height), height)
                to = slice(k * chunk + m * height, k * chunk + (m + 1) * height)
                lhs_ref[to, :] = basis_ref[rows, :]

    for k, piece in enumerate((p0, p1, p2, p3)):
        rhs_ref[k * depth : (k + 1) * depth, :] = piece[...]
    product = jnp.dot(lhs_ref[...], rhs_ref[...], preferred_element_type=jnp.float32)
    for k, out in enumerate(outs):
        out[...] = product[k * chunk : (k + 1) * chunk, :].astype(out.dtype)


def product(axis, distances, where, basis, slab, received):
    rows, width = received[0].shape
    count = basis.shape[0]
    chunk = count // SIDE
    tiles = width // TILE
    depth = SIDE * rows
    height = chunk * len(distances)
    return pl.pallas_call(
        functools.partial(product_kernel, axis, distances),
        grid_spec=pltpu.PrefetchScalarGridSpec(
            num_scalar_prefetch=1,
            grid=(tiles,),
            in_specs=[
                pl.BlockSpec(basis.shape, lambda t, s: (0, 0)),
                pl.BlockSpec((rows, TILE), lambda t, s: (0, (axis * SIDE + s[axis]) * tiles + t)),
            ]
            + [pl.BlockSpec((rows, TILE), lambda t, s: (0, t))] * 3,
            out_specs=[pl.BlockSpec((chunk, TILE), lambda t, s: (0, t))] * len(distances),
            scratch_shapes=[
                pltpu.VMEM((height, depth), jnp.bfloat16),
                pltpu.VMEM((depth, TILE), jnp.bfloat16),
            ],
        ),
        out_shape=[
            jax.ShapeDtypeStruct((chunk, width), jnp.bfloat16 if distance else jnp.float32) for distance in distances
        ],
        compiler_params=pltpu.CompilerParams(vmem_limit_bytes=VMEM),
        cost_estimate=pl.CostEstimate(flops=1, bytes_accessed=1, transcendentals=0),
        name="product",
    )(where, basis, slab, *received)


def collect_kernel(own_ref, g1, g2, g3, *outs):
    total = own_ref[...]
    for got in (g1, g2, g3):
        total = total + got[...].astype(jnp.float32)
    height = outs[0].shape[0]
    for k, out in enumerate(outs):
        out[...] = total[k * height : (k + 1) * height, :].astype(out.dtype)


def collect(own, got, first, blocks):
    chunk, width = own.shape
    height = chunk // SIDE
    rows = height * blocks
    return pl.pallas_call(
        collect_kernel,
        grid=(width // TILE,),
        in_specs=[pl.BlockSpec((rows, TILE), lambda t: (first // blocks, t))] * 4,
        out_specs=[pl.BlockSpec((height, TILE), lambda t: (0, t))] * blocks,
        out_shape=[jax.ShapeDtypeStruct((height, width), jnp.bfloat16)] * blocks,
        compiler_params=pltpu.CompilerParams(vmem_limit_bytes=VMEM),
        cost_estimate=pl.CostEstimate(flops=1, bytes_accessed=1, transcendentals=0),
        name="collect",
    )(own, *got)


PERMS = (x_perm, y_perm)


def shift(value, axis, distance):
    return lax.ppermute(value, "rows", PERMS[axis](lambda q: (q + distance) % SIDE))


def per_device(slab, sign_bits, sampled):
    rows, cols = slab.shape
    count = sampled.shape[0]
    col_devices = lax.axis_size("cols")
    row_devices = lax.axis_size("rows")
    total_rows = rows * row_devices
    share = count // col_devices
    row_index = lax.axis_index("rows")
    places = (row_index % SIDE, row_index // SIDE)
    where = jnp.stack((*places, lax.axis_index("cols"))).astype(jnp.int32)
    width = cols // (2 * SIDE)
    starts = (0, cols // 2)

    def block(source, axis, distance, first=0, size=width):
        start = starts[axis] + (places[axis] + distance) % SIDE * width + first
        return lax.dynamic_slice(source, (0, start), (rows, size))

    slab_x, x_far = lax.optimization_barrier((slab, block(slab, 0, 2)))
    x_far = shift(x_far, 0, 2)
    slab_now, y_far = lax.optimization_barrier((slab_x, block(slab_x, 1, 2)))
    y_far = shift(y_far, 1, 2)

    partial = local_sketch(slab_now, sign_bits, sampled)
    parts = lax.all_to_all(partial, "cols", 0, 0, tiled=True)
    sketch = jnp.sum(parts.reshape(col_devices, share, rows), axis=0)

    def near_blocks(axis):
        return [block(slab_now, axis, distance) for distance in (1, 3)]

    def send_near(blocks, axis):
        return [shift(part, axis, distance) for part, distance in zip(blocks, (1, 3))]

    x_sketch = [sketch] + [shift(sketch, 0, distance) for distance in DISTANCES]
    x_near, x_sketch, x_far = lax.optimization_barrier((near_blocks(0), x_sketch, x_far))
    x_near = send_near(x_near, 0)
    x_squares = sum(jnp.sum(part * part, axis=1, keepdims=True) for part in x_sketch)
    sent = jnp.concatenate([sketch, jnp.broadcast_to(x_squares, (share, 128))], axis=1)
    y_sketch = [sent] + [shift(sent, 1, distance) for distance in DISTANCES]
    y_near, y_sketch, y_far = lax.optimization_barrier((near_blocks(1), y_sketch, y_far))
    y_near = send_near(y_near, 1)
    squares = sum(part[:, rows : rows + 1] for part in y_sketch)
    scale = lax.rsqrt(squares / total_rows + EPSILON)

    bases = []
    for sketches in (x_sketch, y_sketch):
        joined = jnp.concatenate([(part[:, :rows] * scale).astype(jnp.bfloat16) for part in sketches], axis=1)
        bases.append(joined)
    bases[0] = lax.all_to_all(jnp.tile(bases[0], (col_devices, 1)), "cols", 0, 0, tiled=True)
    for mask in (2, 6, 1):
        other = lax.ppermute(bases[1], "cols", [(k, k ^ mask) for k in range(col_devices)])
        bases[1] = jnp.concatenate([bases[1], other], axis=0)

    x_received, y_received = (*x_near, x_far), (*y_near, y_far)
    x_own, *sends = product(0, (0,) + DISTANCES, where, bases[0], slab, x_received)
    x_got = [shift(send, 1, distance) for send, distance in zip(sends, DISTANCES)]
    sends = product(1, (1, 3), where, bases[1], slab, y_received)
    y_got = [shift(send, 0, distance) for send, distance in zip(sends, DISTANCES)]
    y_basis, x_got[0] = lax.optimization_barrier((bases[1], x_got[0]))
    y_own, y_send = product(1, (0, 2), where, y_basis, slab, y_received)
    y_got.append(shift(y_send, 0, 2))
    out = ()
    for axis, own, got in ((0, x_own, x_got), (1, y_own, y_got)):
        (far,) = collect(own, got, 2, 1)
        far = shift(far, axis, 2)
        near = collect(own, got, 0, 2)
        near = [shift(part, axis, distance) for part, distance in zip(near, (1, 3))]
        out = (assemble(axis, where, own, got, (*near, far), out),)
    return out[0]


def solution(mesh):
    return jax.shard_map(
        per_device,
        mesh=mesh,
        in_specs=(P("rows", "cols"), P("cols"), P()),
        out_specs=P("rows", "cols"),
        check_vma=False,
    )
```
